128 devices in a mesh: grp: 2 (over core), dev: 64 (over z, x, y).
Axes of the slice: x: 4, y: 4, z: 4, core: 2. Of those that a mesh axis runs over, the one named last changes fastest.
Arguments:
- queries: bfloat16 [2048, 8192], P(('grp', 'dev')), may hold values from -27 to 27
- cache_keys: bfloat16 [2048, 32, 512], P(('grp', 'dev')), may hold values from -6 to 6
- cache_values: bfloat16 [2048, 32, 512], P(('grp', 'dev')), may hold values from -6 to 6
- own_len: int32 [2048], P(('grp', 'dev')), may hold values from 2 to 32, as said below
- ext_keys: bfloat16 [2048, 32, 512], P(('grp', 'dev')), may hold values from -6 to 6
- ext_values: bfloat16 [2048, 32, 512], P(('grp', 'dev')), may hold values from -6 to 6
- ext_len: int32 [2048], P(('grp', 'dev')), may hold values from 0 to 32, as said below
- new_key: bfloat16 [2048, 512], P(('grp', 'dev')), may hold values from -6 to 6
- new_value: bfloat16 [2048, 512], P(('grp', 'dev')), may hold values from -6 to 6
- moe_input: bfloat16 [2048, 4096], P(('grp', 'dev')), may hold values from -6 to 6
- expert_ids: int32 [2048, 8], P(('grp', 'dev')), may hold values from 0 to 127, all different within a row; in each aligned block of 16 rows (0 to 15, 16 to 31, ...) at most 2 rows name the same one
- route_scores: float32 [2048, 8], P(('grp', 'dev')), may hold values from 0.05 to 1
- w_gate: bfloat16 [128, 4096, 768], P(('grp', 'dev')), may hold values from -0.09375 to 0.09375
- w_up: bfloat16 [128, 4096, 768], P(('grp', 'dev')), may hold values from -0.09375 to 0.09375
- w_down: bfloat16 [128, 768, 4096], P(('grp', 'dev')), may hold values from -0.21875 to 0.21875
Outputs:
- attention_out: bfloat16 [2048, 8192], P(('grp', 'dev'))
- moe_out: bfloat16 [2048, 4096], P(('grp', 'dev'))
The draws below stay inside these ranges and needn't reach their ends.
Inputs may be any that keep to these rules, and one draw needn't show every extreme that they name: own_len[r] is 32 wherever ext_len[p(r)] is positive; some row of every device has 32. ext_len at a position is zero where the paired row has no continuation; the first position of every device has 32. `expert_ids`: each row names 8 different experts; among the rows of one device no expert is named more than 2 times, a bound that some block reaches.
All inputs are finite; a program needn't handle non-finite values.
Results may differ from the reference program's by a relative error of at most 0.008.
Values may be sent and summed in bfloat16 or wider, within the bound.
No kernel may reach another device: no remote copies, remote signals or barrier semaphores. Data moves between devices by JAX's collectives and lax.ppermute only.
A program may use at most 128 MiB of HBM per device.

```python
import math
import jax
import jax.numpy as jnp
import numpy as np
from jax import lax

D = 4096
QH = 64
KVH = 4
HD = 128
TOPK = 8
MOE_FF = 768
SLOTS = 32
ROWS_DEV = 16
EXPERTS = 128
ROWS = 2048
CAP = 2
N_GRP = 2
N_DEV = 64


def split_plan(key):
    split_flag = jax.random.randint(jax.random.fold_in(key, 11), (ROWS,), 0, 2)
    lengths = jax.random.randint(jax.random.fold_in(key, 12), (ROWS,), 1, SLOTS + 1)
    first = jnp.arange(ROWS, dtype=jnp.int32) % ROWS_DEV == 0
    split_flag = jnp.where(first, 1, split_flag)
    far_len = jnp.where(first, SLOTS, lengths) * split_flag
    paired = far_len.reshape(ROWS // (2 * ROWS_DEV), 2, ROWS_DEV)[:, ::-1].reshape(ROWS)
    own_random = jax.random.randint(jax.random.fold_in(key, 13), (ROWS,), 2, SLOTS + 1)
    own_len = jnp.where(paired > 0, SLOTS, own_random)
    return (own_len.astype(jnp.int32), far_len.astype(jnp.int32))


def draw_own_len(key, part):
    own_len, far_len = split_plan(key)
    return own_len


def draw_ext_len(key, part):
    own_len, far_len = split_plan(key)
    return far_len


def draw_cache_keys(key, part):
    key = jax.random.fold_in(key, 3)
    base = jax.random.normal(key, (ROWS, SLOTS, KVH * HD), jnp.float32)
    return jnp.clip(base, -6.0, 6.0).astype(jnp.bfloat16)


def draw_queries(key, part):
    key = jax.random.fold_in(key, 5)
    base = jnp.clip(jax.random.normal(key, (ROWS, QH * HD), jnp.float32), -6.0, 6.0)
    return base.astype(jnp.bfloat16)


def shard_levels(key, shape, cuts, smallest, top_value):
    level, own = 1.0, jax.random.fold_in(key, 6)
    for position, shards_of in cuts:
        heights = jnp.exp(jax.random.uniform(jax.random.fold_in(own, position), (shards_of,), jnp.float32, smallest / len(cuts), top_value / len(cuts)))
        level = level * jnp.repeat(heights, shape[position] // shards_of).reshape([-1 if axis == position else 1 for axis in range(len(shape))])
    return level


def deal_out(stream_key, own, number, rows, number_of, top, reach, lean):
    ranking = jax.random.permutation(stream_key, number_of)
    packed, common = portions_of(number_of, rows * top, reach, lean, True), portions_of(number_of, rows * top, reach, lean, False)
    places = jnp.arange(number_of)

    def named(sizes, offset_by):
        used = int((sizes > 0).sum())
        fixed = max(1, used // 4)
        moved = fixed + (places - fixed + offset_by * (used - fixed)) % max(1, number_of - fixed)
        return jnp.zeros((number_of,), jnp.int32).at[ranking[jnp.where(places < fixed, places, moved)]].set(jnp.asarray(sizes, jnp.int32))

    sizes = jnp.where(number % 4 == 0, named(packed, number // 4), named(common, number - number // 4 - 1))
    mixed = jax.random.permutation(jax.random.fold_in(own, 3), number_of)
    source_of, sink = mixed[0:number_of // 2 * 2:2], mixed[1:number_of // 2 * 2:2]
    margin = jnp.minimum(sizes[source_of] - 1, reach - sizes[sink]) // 2
    margin = jnp.where((source_of == ranking[0]) | (sink == ranking[0]) | (sizes[sink] == 0), 0, jnp.maximum(margin, 0))
    moved = jax.random.randint(jax.random.fold_in(own, 4), (number_of // 2,), 0, 1 << 20) % (margin + 1)
    sizes = sizes.at[source_of].add(-moved).at[sink].add(moved)
    members = jnp.searchsorted(jnp.cumsum(sizes), jnp.arange(rows * top), side="right").astype(jnp.int32)
    listing = members.reshape(top, rows).T
    listing = listing[jax.random.permutation(jax.random.fold_in(own, 1), rows)]
    offset_by = jax.random.randint(jax.random.fold_in(own, 2), (rows, 1), 0, top)
    return jnp.take_along_axis(listing, (jnp.arange(top)[None, :] + offset_by) % top, axis=1)


def portions_of(number_of, total, limit, slope, full):
    weights = [(1 << 20) // math.isqrt(rank ** slope) + 1 for rank in range(1, number_of + 1)]
    largest = limit if full else min(limit, max(-(-total // number_of), total * weights[0] // sum(weights)))
    least = 1 if total - largest >= number_of - 1 else 0
    given, surplus = [largest] + [least] * (number_of - 1), total - largest - least * (number_of - 1)
    while surplus > 0:
        free = [i for i in range(1, number_of) if given[i] < largest] or [i for i in range(1, number_of) if given[i] < limit]
        whole, remaining = sum([weights[i] for i in free]), surplus
        for i in free:
            extra = min(limit - given[i], max(1, remaining * weights[i] // whole), surplus)
            given[i] = given[i] + extra
            surplus = surplus - extra
    return np.array(given)


def scatter_about(key, shape, deviation, most, cuts=(), held_as=jnp.bfloat16):
    values = jax.random.normal(key, shape, jnp.float32) * deviation
    if len(cuts) > 0:
        values = shard_levels(key, shape, cuts, -0.22, 0.18) * values
    return jnp.clip(values, min=-most, max=most).astype(held_as)


def setup_inputs(seed: int = 0) -> dict:
    streams_of = jax.random.split(jax.random.key(seed), 16)
    queries = draw_queries(jax.random.fold_in(streams_of[15], 71), 0)
    cache_keys = draw_cache_keys(jax.random.fold_in(streams_of[15], 71), 0)
    cache_values = scatter_about(streams_of[2], (ROWS, SLOTS, KVH * HD), 1.0, 6.0, ((0, 128),))
    own_len = draw_own_len(jax.random.fold_in(streams_of[15], 71), 0)
    ext_keys = scatter_about(streams_of[4], (ROWS, SLOTS, KVH * HD), 1.0, 6.0, ((0, 128),))
    ext_values = scatter_about(streams_of[5], (ROWS, SLOTS, KVH * HD), 1.0, 6.0, ((0, 128),))
    ext_len = draw_ext_len(jax.random.fold_in(streams_of[15], 71), 0)
    new_key = scatter_about(streams_of[7], (ROWS, KVH * HD), 1.0, 6.0, ((0, 128),))
    new_value = scatter_about(streams_of[8], (ROWS, KVH * HD), 1.0, 6.0, ((0, 128),))
    moe_input = scatter_about(streams_of[9], (ROWS, D), 1.0, 6.0, ((0, 128),))
    expert_ids_keys = jax.random.split(jax.random.fold_in(streams_of[10], 1), ROWS // ROWS_DEV)
    expert_ids_turns = jax.random.permutation(jax.random.fold_in(streams_of[10], 3), ROWS // ROWS_DEV)
    expert_ids = jax.vmap(lambda own, number: deal_out(jax.random.fold_in(streams_of[10], 2), own, number, ROWS_DEV, EXPERTS, TOPK, CAP, 2))(expert_ids_keys, expert_ids_turns).reshape((ROWS, TOPK))
    route_scores = jnp.clip(jnp.exp(math.log(1.0) - 2.9957323 * jax.random.uniform(streams_of[11], (ROWS, TOPK), jnp.float32) ** shard_levels(streams_of[11], (ROWS, TOPK), ((0, 128),), -0.2, 0.2)), 0.05, 1.0)
    w_gate = scatter_about(streams_of[12], (EXPERTS, D, MOE_FF), D ** -0.5, 0.09375, ((0, 128),))
    w_up = scatter_about(streams_of[13], (EXPERTS, D, MOE_FF), D ** -0.5, 0.09375, ((0, 128),))
    w_down = scatter_about(streams_of[14], (EXPERTS, MOE_FF, D), MOE_FF ** -0.5, 0.21875, ((0, 128),))
    return {"queries": queries, "cache_keys": cache_keys, "cache_values": cache_values, "own_len": own_len, "ext_keys": ext_keys, "ext_values": ext_values, "ext_len": ext_len, "new_key": new_key, "new_value": new_value, "moe_input": moe_input, "expert_ids": expert_ids, "route_scores": route_scores, "w_gate": w_gate, "w_up": w_up, "w_down": w_down}


def partner_view(array):
    shaped = array.reshape((array.shape[0] // (2 * ROWS_DEV), 2, ROWS_DEV) + array.shape[1:])
    return shaped[:, ::-1].reshape(array.shape)

def attend(block):
    queries, keys, values, far_keys, far_values, new_key, new_value, own_len, far_len = block
    count = queries.shape[0]
    groups = QH // KVH
    width = 2 * SLOTS + 1
    all_keys = jnp.concatenate([keys, far_keys, new_key[:, None, :]], axis=1).astype(jnp.float32).reshape(count, width, KVH, HD)
    all_values = jnp.concatenate([values, far_values, new_value[:, None, :]], axis=1).astype(jnp.float32).reshape(count, width, KVH, HD)
    query_flat = queries.astype(jnp.float32).reshape(count, KVH, groups, HD)
    positions = jnp.arange(width, dtype=jnp.int32)[None, :]
    live_slots = (positions < own_len[:, None]) | (positions >= SLOTS) & (positions - SLOTS < far_len[:, None]) | (positions == 2 * SLOTS)
    scores = jnp.einsum('rkgh,rskh->rkgs', query_flat, all_keys) / jnp.sqrt(jnp.float32(HD))
    scores = jnp.where(live_slots[:, None, None, :], scores, -jnp.inf)
    row_max = lax.optimization_barrier(jnp.max(scores, axis=-1, keepdims=True))
    weights = jnp.exp(scores - row_max)
    row_total = lax.optimization_barrier(jnp.sum(weights, axis=-1))
    result = jnp.einsum('rkgs,rskh->rkgh', weights, all_values) / row_total[..., None]
    return result.reshape(count, QH * HD).astype(jnp.bfloat16)

def reference(queries, cache_keys, cache_values, own_len, ext_keys, ext_values, ext_len, new_key, new_value, moe_input, expert_ids, route_scores, w_gate, w_up, w_down):
    device_count = N_GRP * N_DEV
    far_keys = partner_view(ext_keys)
    far_values = partner_view(ext_values)
    far_len = partner_view(ext_len)

    def blocked(array):
        return array.reshape((device_count, ROWS_DEV) + array.shape[1:])
    pieces = (queries, cache_keys, cache_values, far_keys, far_values, new_key, new_value, own_len, far_len)
    attention_out = lax.map(attend, tuple((blocked(piece) for piece in pieces))).reshape(ROWS, QH * HD)
    per_device = ROWS_DEV * TOPK
    flat_ids = expert_ids.reshape(device_count, per_device)
    onehot = (flat_ids[..., None] == jnp.arange(EXPERTS, dtype=jnp.int32)[None, None, :]).astype(jnp.int32)
    slot_rank = lax.optimization_barrier(jnp.sum(jnp.cumsum(onehot, axis=1) * onehot, axis=2)) - 1
    device_ids = jnp.arange(device_count, dtype=jnp.int32)[:, None]
    columns = (device_ids * CAP + slot_rank).astype(jnp.int32)
    row_ids = (device_ids * ROWS_DEV + jnp.arange(per_device, dtype=jnp.int32)[None, :] // TOPK).astype(jnp.int32)
    route_weights = (route_scores / lax.optimization_barrier(jnp.sum(route_scores, axis=1, keepdims=True))).reshape(device_count, per_device)
    table_rows = jnp.full((EXPERTS, device_count * CAP), ROWS, jnp.int32).at[flat_ids, columns].set(row_ids)
    table_weights = jnp.zeros((EXPERTS, device_count * CAP), jnp.float32).at[flat_ids, columns].set(route_weights)
    padded = jnp.concatenate([moe_input, jnp.zeros((1, D), jnp.bfloat16)], axis=0)

    def one_expert(carry, inputs):
        rows_here, weights_here, gate_w, up_w, down_w = inputs
        chosen = padded[rows_here]
        gate_act = jnp.dot(chosen, gate_w, preferred_element_type=jnp.float32)
        up_act = jnp.dot(chosen, up_w, preferred_element_type=jnp.float32)
        expert_hidden = (jax.nn.silu(gate_act) * up_act).astype(jnp.bfloat16)
        expert_out = jnp.dot(expert_hidden, down_w, preferred_element_type=jnp.float32).astype(jnp.bfloat16)
        carry = carry.at[rows_here].add(weights_here[:, None] * expert_out.astype(jnp.float32))
        return (carry, None)
    summed, unused = lax.scan(one_expert, jnp.zeros((ROWS + 1, D), jnp.float32), (table_rows, table_weights, w_gate, w_up, w_down))
    moe_out = summed[:ROWS].astype(jnp.bfloat16)
    return (attention_out, moe_out)
```

```python
import jax
import jax.numpy as jnp
from jax import lax
from jax.experimental import pallas as pl
from jax.experimental.pallas import tpu as pltpu
from jax.sharding import PartitionSpec as P

QH = 64
KVH = 4
HD = 128
DMODEL = 4096
FF = 768
TOPK = 8
EXPERTS = 128
ROW_BLOCK = 16
LANES = 128
GROUPS = 4
CHUNK = 64
PREP_PIECES = 4
COMBINE_STEPS = 4


def partner(block, axis, apart):
    count = lax.axis_size(axis)
    route = []
    for low in range(count):
        high = low | 1 << apart
        if high != low and high < count:
            route += [(low, high), (high, low)]
    return lax.ppermute(block, axis, route)


def partial_softmax(queries, keys, values, live_slots):
    row_count = queries.shape[0]
    groups = QH // KVH
    query_flat = queries.astype(jnp.float32).reshape(row_count, KVH, groups, HD)
    key_flat = keys.astype(jnp.float32).reshape(row_count, keys.shape[1], KVH, HD)
    value_flat = values.astype(jnp.float32).reshape(row_count, values.shape[1], KVH, HD)
    scores = jnp.einsum("rkgh,rskh->rkgs", query_flat, key_flat) / jnp.sqrt(jnp.float32(HD))
    live_mask = live_slots[:, None, None, :]
    row_max = jnp.max(jnp.where(live_mask, scores, -jnp.inf), axis=-1)
    row_max = jnp.where(jnp.isfinite(row_max), row_max, -1e30)
    weights = jnp.where(live_mask, jnp.exp(scores - row_max[..., None]), 0.0)
    row_total = jnp.sum(weights, axis=-1)
    numerator = jnp.einsum("rkgs,rskh->rkgh", weights, value_flat)
    return (
        row_max.reshape(row_count, QH),
        row_total.reshape(row_count, QH),
        numerator.reshape(row_count, QH, HD),
    )


def merge_parts(first, second):
    max_one, total_one, numer_one = first
    max_two, total_two, numer_two = second
    largest = jnp.maximum(max_one, max_two)
    scale_one = jnp.exp(max_one - largest)
    scale_two = jnp.exp(max_two - largest)
    row_total = total_one * scale_one + total_two * scale_two
    numerator = numer_one * scale_one[..., None] + numer_two * scale_two[..., None]
    merged = numerator / row_total[..., None]
    return merged.reshape(merged.shape[0], -1).astype(jnp.bfloat16)


def slot_index_kernel(ids_ref, x_ref, out_ref, stack_ref, first_ref, second_ref, sem):
    lane = lax.broadcasted_iota(jnp.int32, (ROW_BLOCK, LANES), 1)
    row = lax.broadcasted_iota(jnp.int32, (ROW_BLOCK, LANES), 0)
    spread = (lane % ROW_BLOCK == row).astype(jnp.bfloat16)
    ids = ids_ref[...].astype(jnp.float32).astype(jnp.bfloat16)
    named = lax.dot_general(ids, spread, (((0,), (0,)), ((), ())), preferred_element_type=jnp.float32)
    expert = lax.broadcasted_iota(jnp.int32, (EXPERTS, LANES), 0).astype(jnp.float32)
    chosen = jnp.zeros((EXPERTS, LANES), jnp.float32)
    for choice in range(TOPK):
        chosen = jnp.where(expert == named[choice : choice + 1, :], 1.0, chosen)
    from_lane = lax.broadcasted_iota(jnp.int32, (LANES, LANES), 0)
    to_lane = lax.broadcasted_iota(jnp.int32, (LANES, LANES), 1)
    earlier = (from_lane // ROW_BLOCK == to_lane // ROW_BLOCK) & (from_lane < to_lane)
    rank = jnp.dot(
        chosen.astype(jnp.bfloat16), earlier.astype(jnp.float32).astype(jnp.bfloat16),
        preferred_element_type=jnp.float32,
    )
    first_ref[...] = jnp.where(rank == 0.0, chosen, 0.0)
    second_ref[...] = jnp.where(rank == 1.0, chosen, 0.0)
    for tile in range(8):
        for group in range(GROUPS):
            column = (group * 8 + tile) * LANES
            stack_ref[tile * 16 : (tile + 1) * 16, group * LANES : (group + 1) * LANES] = x_ref[
                :, column : column + LANES
            ]
    sub = lax.broadcasted_iota(jnp.int32, (16, LANES), 0)
    sub_lane = lax.broadcasted_iota(jnp.int32, (16, LANES), 1)
    own_tile = sub_lane // ROW_BLOCK == sub // 2
    mask_first = jnp.where(own_tile & (sub % 2 == 0), 1.0, 0.0)
    mask_second = jnp.where(own_tile & (sub % 2 == 1), 1.0, 0.0)
    stacked = stack_ref[...]
    copies = []
    per_piece = EXPERTS // PREP_PIECES
    for piece in range(PREP_PIECES):
        pieces = []
        for expert_at in range(piece * per_piece, (piece + 1) * per_piece):
            one = first_ref[expert_at : expert_at + 1, :]
            two = second_ref[expert_at : expert_at + 1, :]
            pieces.append((one * mask_first + two * mask_second).astype(jnp.bfloat16))
        picker = jnp.concatenate(pieces, axis=0)
        rows = jnp.dot(picker, stacked, preferred_element_type=jnp.float32).astype(jnp.bfloat16)
        for group in range(GROUPS):
            out_ref[
                piece * per_piece : (piece + 1) * per_piece, group * 16 : (group + 1) * 16, :
            ] = rows[:, group * LANES : (group + 1) * LANES].reshape(per_piece, 16, LANES)


def weight_table_kernel(ids_ref, scores_ref, table_ref):
    scores = scores_ref[...]
    shares = scores / jnp.sum(scores, axis=1, keepdims=True)
    ids = ids_ref[...]
    expert = lax.broadcasted_iota(jnp.int32, (ROW_BLOCK, EXPERTS), 1)
    chosen = jnp.zeros((ROW_BLOCK, EXPERTS), jnp.float32)
    share_of = jnp.zeros((ROW_BLOCK, EXPERTS), jnp.float32)
    for choice in range(TOPK):
        same = ids[:, choice : choice + 1] == expert
        chosen = jnp.where(same, 1.0, chosen)
        share_of = jnp.where(same, shares[:, choice : choice + 1], share_of)
    below = lax.broadcasted_iota(jnp.int32, (ROW_BLOCK, ROW_BLOCK), 1)
    above = lax.broadcasted_iota(jnp.int32, (ROW_BLOCK, ROW_BLOCK), 0)
    earlier = jnp.where(below < above, 1.0, 0.0).astype(jnp.bfloat16)
    rank = jnp.dot(earlier, chosen.astype(jnp.bfloat16), preferred_element_type=jnp.float32)
    slot_shares = jnp.concatenate(
        [jnp.where(rank == 0.0, share_of, 0.0), jnp.where(rank == 1.0, share_of, 0.0)], axis=1
    )
    high = slot_shares.astype(jnp.bfloat16)
    low = (slot_shares - high.astype(jnp.float32)).astype(jnp.bfloat16)
    both = jnp.concatenate([high, low], axis=0)
    piece = 512
    for start in range(0, EXPERTS * 16, piece):
        source = lax.broadcasted_iota(jnp.int32, (2 * EXPERTS, piece), 0)
        target = lax.broadcasted_iota(jnp.int32, (2 * EXPERTS, piece), 1) + start
        wanted = (target % 2) * EXPERTS + target // 16
        spread = jnp.where(source == wanted, 1.0, 0.0).astype(jnp.bfloat16)
        wide = jnp.dot(both, spread, preferred_element_type=jnp.float32)
        tile_of = (lax.broadcasted_iota(jnp.int32, (ROW_BLOCK, piece), 1) // 2) % 8
        for part in range(2):
            rows = wide[part * ROW_BLOCK : (part + 1) * ROW_BLOCK, :]
            for tile in range(8):
                at = part * LANES + tile * ROW_BLOCK
                table_ref[at : at + ROW_BLOCK, start : start + piece] = jnp.where(
                    tile_of == tile, rows, 0.0
                ).astype(jnp.bfloat16)


def ffn_kernel(
    x_hbm, gate_hbm, up_hbm, down_hbm, out_hbm,
    x_ref, gate_ref, up_ref, down_ref, y_ref, rows_ref, gate_acc, up_acc, x_sem, gate_sem, up_sem, down_sem, y_sem,
):
    span = DMODEL // GROUPS

    def x_copy(group):
        return pltpu.make_async_copy(
            x_hbm.at[:, pl.ds(group * 16, 16), :], x_ref.at[group], x_sem.at[group]
        )

    def gate_copy(group):
        part = pl.ds(group * span, span)
        return pltpu.make_async_copy(gate_hbm.at[0, part, :], gate_ref.at[part, :], gate_sem.at[group])

    def up_copy(group):
        part = pl.ds(group * span, span)
        return pltpu.make_async_copy(up_hbm.at[0, part, :], up_ref.at[part, :], up_sem.at[group])

    def down_copy(group):
        part = pl.ds(group * span, span)
        return pltpu.make_async_copy(down_hbm.at[0, :, part], down_ref.at[group], down_sem.at[group])

    def y_copy(group):
        return pltpu.make_async_copy(
            y_ref.at[group], out_hbm.at[:, pl.ds(group * 16, 16), :], y_sem.at[group]
        )

    for group in range(GROUPS):
        x_copy(group).start()
        gate_copy(group).start()
        up_copy(group).start()
    for group in range(GROUPS):
        down_copy(group).start()

    out_row = lax.broadcasted_iota(jnp.int32, (LANES, LANES), 0)
    in_row = lax.broadcasted_iota(jnp.int32, (LANES, LANES), 1)
    gathered_from = (out_row // 2 % 8) * 16 + (out_row // 16) * 2 + out_row % 2
    swap = jnp.where(in_row == gathered_from, 1.0, 0.0).astype(jnp.bfloat16)

    for group in range(GROUPS):
        x_copy(group).wait()
        for block in range(0, 16, 2):
            pair = jnp.concatenate(
                [x_ref[group, (block + i) * 8 : (block + i + 1) * 8].reshape(LANES, LANES) for i in range(2)], axis=1
            )
            moved = jnp.dot(swap, pair, preferred_element_type=jnp.float32).astype(jnp.bfloat16)
            for tile in range(8):
                for i in range(2):
                    rows_ref[
                        (block + i) * 16 : (block + i + 1) * 16, tile * LANES : (tile + 1) * LANES
                    ] = moved[tile * 16 : (tile + 1) * 16, i * LANES : (i + 1) * LANES]
        rows = rows_ref[...]
        gate_copy(group).wait()
        gate_part = jnp.dot(
            rows, gate_ref[group * span : (group + 1) * span, :], preferred_element_type=jnp.float32
        )
        up_copy(group).wait()
        up_part = jnp.dot(
            rows, up_ref[group * span : (group + 1) * span, :], preferred_element_type=jnp.float32
        )
        if group == 0:
            gate_acc[...] = gate_part
            up_acc[...] = up_part
        else:
            gate_acc[...] += gate_part
            up_acc[...] += up_part
    gate = gate_acc[...]
    hidden = (gate / (1.0 + jnp.exp(-gate)) * up_acc[...]).astype(jnp.bfloat16)
    for group in range(GROUPS):
        down_copy(group).wait()
        rows_ref[...] = jnp.dot(hidden, down_ref[group], preferred_element_type=jnp.float32).astype(jnp.bfloat16)
        for block in range(0, 16, 2):
            pair = jnp.concatenate(
                [
                    jnp.concatenate(
                        [
                            rows_ref[(block + i) * 16 : (block + i + 1) * 16, tile * LANES : (tile + 1) * LANES]
                            for tile in range(8)
                        ],
                        axis=0,
                    )
                    for i in range(2)
                ],
                axis=1,
            )
            moved = jnp.dot(swap, pair, preferred_element_type=jnp.float32).astype(jnp.bfloat16)
            for i in range(2):
                y_ref[group, (block + i) * 8 : (block + i + 1) * 8] = moved[
                    :, i * LANES : (i + 1) * LANES
                ].reshape(8, 16, LANES)
        y_copy(group).start()
    for group in range(GROUPS):
        y_copy(group).wait()


def combine_kernel(table_ref, back_ref, out_ref, total_ref):
    step = pl.program_id(0)
    depth = back_ref.shape[0] * 16
    part = jnp.dot(
        table_ref[...],
        jnp.concatenate(
            [back_ref[:, group * 16 : (group + 1) * 16, :].reshape(depth, LANES) for group in range(GROUPS)], axis=1
        ),
        preferred_element_type=jnp.float32,
    )

    @pl.when(step == 0)
    def _():
        total_ref[...] = part

    @pl.when(step > 0)
    def _():
        total_ref[...] += part

    @pl.when(step == pl.num_programs(0) - 1)
    def _():
        summed = total_ref[:LANES, :] + total_ref[LANES:, :]
        for tile in range(8):
            for group in range(GROUPS):
                column = (group * 8 + tile) * LANES
                out_ref[:, column : column + LANES] = summed[
                    tile * 16 : (tile + 1) * 16, group * LANES : (group + 1) * LANES
                ].astype(jnp.bfloat16)


def whole():
    return pl.BlockSpec(memory_space=pltpu.VMEM)


def cost(flops, moved):
    return pl.CostEstimate(flops=flops, bytes_accessed=moved, transcendentals=0)


def experts_of(moe_input, expert_ids, route_scores, w_gate, w_up, w_down):
    exchange = jax.ShapeDtypeStruct((EXPERTS, CHUNK, LANES), jnp.bfloat16)
    outgoing = pl.pallas_call(
        slot_index_kernel,
        out_shape=exchange,
        in_specs=[whole(), whole()],
        out_specs=whole(),
        scratch_shapes=[
            pltpu.VMEM((LANES, GROUPS * LANES), jnp.bfloat16),
            pltpu.VMEM((EXPERTS, LANES), jnp.float32),
            pltpu.VMEM((EXPERTS, LANES), jnp.float32),
            pltpu.SemaphoreType.DMA((PREP_PIECES,)),
        ],
        compiler_params=pltpu.CompilerParams(vmem_limit_bytes=32 << 20),
        cost_estimate=cost(300_000_000, 2_300_000),
        name="dispatch_rows",
    )(expert_ids, moe_input)
    arrived = lax.all_to_all(outgoing, ("grp", "dev"), split_axis=0, concat_axis=0, tiled=True)
    table = pl.pallas_call(
        weight_table_kernel,
        out_shape=jax.ShapeDtypeStruct((2 * LANES, EXPERTS * 16), jnp.bfloat16),
        in_specs=[whole(), whole()],
        out_specs=whole(),
        compiler_params=pltpu.CompilerParams(vmem_limit_bytes=32 << 20),
        cost_estimate=cost(100_000_000, 1_100_000),
        name="route_table",
    )(expert_ids, route_scores)
    anywhere = pl.BlockSpec(memory_space=pl.ANY)
    answers = pl.pallas_call(
        ffn_kernel,
        out_shape=exchange,
        in_specs=[anywhere] * 4,
        out_specs=anywhere,
        scratch_shapes=[
            pltpu.VMEM((GROUPS, EXPERTS, 16, LANES), jnp.bfloat16),
            pltpu.VMEM((DMODEL, FF), jnp.bfloat16),
            pltpu.VMEM((DMODEL, FF), jnp.bfloat16),
            pltpu.VMEM((GROUPS, FF, DMODEL // GROUPS), jnp.bfloat16),
            pltpu.VMEM((GROUPS, EXPERTS, 16, LANES), jnp.bfloat16),
            pltpu.VMEM((2 * EXPERTS, DMODEL // GROUPS), jnp.bfloat16),
            pltpu.VMEM((2 * EXPERTS, FF), jnp.float32),
            pltpu.VMEM((2 * EXPERTS, FF), jnp.float32),
        ]
        + [pltpu.SemaphoreType.DMA((GROUPS,))] * 5,
        compiler_params=pltpu.CompilerParams(vmem_limit_bytes=48 << 20),
        cost_estimate=cost(4_800_000_000, 23_000_000),
        name="expert_ffn",
    )(arrived, w_gate, w_up, w_down)
    returned = lax.all_to_all(answers, ("grp", "dev"), split_axis=0, concat_axis=0, tiled=True)
    per_step = EXPERTS // COMBINE_STEPS
    return pl.pallas_call(
        combine_kernel,
        grid=(COMBINE_STEPS,),
        out_shape=jax.ShapeDtypeStruct((ROW_BLOCK, DMODEL), jnp.bfloat16),
        in_specs=[
            pl.BlockSpec((2 * LANES, per_step * 16), lambda step: (0, step)),
            pl.BlockSpec((per_step, CHUNK, LANES), lambda step: (step, 0, 0)),
        ],
        out_specs=pl.BlockSpec((ROW_BLOCK, DMODEL), lambda step: (0, 0)),
        scratch_shapes=[pltpu.VMEM((2 * LANES, GROUPS * LANES), jnp.float32)],
        compiler_params=pltpu.CompilerParams(vmem_limit_bytes=32 << 20),
        cost_estimate=cost(540_000_000, 3_300_000),
        name="weighted_sum",
    )(table, returned)


def body(
    queries,
    cache_keys,
    cache_values,
    own_len,
    ext_keys,
    ext_values,
    ext_len,
    new_key,
    new_value,
    moe_input,
    expert_ids,
    route_scores,
    w_gate,
    w_up,
    w_down,
):
    slot_count = cache_keys.shape[1]
    positions = jnp.arange(slot_count + 1, dtype=jnp.int32)[None, :]
    own_live = (positions < own_len[:, None]) | (positions == slot_count)
    own_keys = jnp.concatenate([cache_keys, new_key[:, None, :]], axis=1)
    own_values = jnp.concatenate([cache_values, new_value[:, None, :]], axis=1)
    own_part = partial_softmax(queries, own_keys, own_values, own_live)
    far_positions = positions[:, :slot_count]
    far_keys, far_values, far_len = partner((ext_keys, ext_values, ext_len), "dev", 0)
    far_part = partial_softmax(queries, far_keys, far_values, far_positions < far_len[:, None])
    attention_out = merge_parts(own_part, far_part)
    moe_out = experts_of(moe_input, expert_ids, route_scores, w_gate, w_up, w_down)
    return (attention_out, moe_out)


def solution(mesh):
    placed = (
        P(("grp", "dev"), None),
        P(("grp", "dev"), None, None),
        P(("grp", "dev"), None, None),
        P(("grp", "dev")),
        P(("grp", "dev"), None, None),
        P(("grp", "dev"), None, None),
        P(("grp", "dev")),
        P(("grp", "dev"), None),
        P(("grp", "dev"), None),
        P(("grp", "dev"), None),
        P(("grp", "dev"), None),
        P(("grp", "dev"), None),
        P(("grp", "dev"), None, None),
        P(("grp", "dev"), None, None),
        P(("grp", "dev"), None, None),
    )
    return jax.shard_map(
        body,
        mesh=mesh,
        in_specs=placed,
        out_specs=(P(("grp", "dev"), None), P(("grp", "dev"), None)),
        check_vma=False,
    )
```

```python
import jax
import jax.numpy as jnp
from jax import lax
from jax.experimental import pallas as pl
from jax.experimental.pallas import tpu as pltpu
from jax.sharding import PartitionSpec as P

QH = 64
KVH = 4
HD = 128
DMODEL = 4096
FF = 768
TOPK = 8
EXPERTS = 128
ROW_BLOCK = 16
LANES = 128
GROUPS = 4
CHUNK = 64
PREP_PIECES = 8
FFN_PIECES = 8
FFN_AHEAD = 3
ALL_VMEM = 60 << 20
FFN_VMEM = 48 << 20
TIE_VMEM = 16 << 20
LATE_TIE_VMEM = 16 << 20


def partner(block, axis, apart):
    count = lax.axis_size(axis)
    route = []
    for low in range(count):
        high = low | 1 << apart
        if high != low and high < count:
            route += [(low, high), (high, low)]
    return lax.ppermute(block, axis, route)


def partial_softmax(queries, keys, values, live_slots):
    row_count = queries.shape[0]
    groups = QH // KVH
    query_flat = queries.astype(jnp.float32).reshape(row_count, KVH, groups, HD)
    key_flat = keys.astype(jnp.float32).reshape(row_count, keys.shape[1], KVH, HD)
    value_flat = values.astype(jnp.float32).reshape(row_count, values.shape[1], KVH, HD)
    scores = jnp.einsum("rkgh,rskh->rkgs", query_flat, key_flat) / jnp.sqrt(jnp.float32(HD))
    live_mask = live_slots[:, None, None, :]
    row_max = jnp.max(jnp.where(live_mask, scores, -jnp.inf), axis=-1)
    row_max = jnp.where(jnp.isfinite(row_max), row_max, -1e30)
    weights = jnp.where(live_mask, jnp.exp(scores - row_max[..., None]), 0.0)
    row_total = jnp.sum(weights, axis=-1)
    numerator = jnp.einsum("rkgs,rskh->rkgh", weights, value_flat)
    return (
        row_max.reshape(row_count, QH),
        row_total.reshape(row_count, QH),
        numerator.reshape(row_count, QH, HD),
    )


def packed_part(part):
    row_max, row_total, numerator = part
    live = row_total > 0.0
    safe = jnp.where(live, row_total, 1.0)
    level = jnp.where(live, row_max + jnp.log(safe), -1e30)
    high = lax.reduce_precision(level, 8, 7)
    middle = lax.reduce_precision(level - high, 8, 7)
    low = level - high - middle
    levels = jnp.concatenate([high, middle, low, jnp.zeros_like(low)], axis=1)
    mean = numerator / safe[..., None]
    return jnp.concatenate([mean, levels.reshape(-1, 2, HD)], axis=1).astype(jnp.bfloat16)


def unpacked_part(packed):
    levels = packed[:, QH:].reshape(-1, 4, QH).astype(jnp.float32)
    return levels[:, 0] + levels[:, 1] + levels[:, 2], packed[:, :QH]


def tie_kernel(one_ref, two_ref, one_out_ref, two_out_ref):
    pass


def tied(one, two, limit):
    anywhere = pl.BlockSpec(memory_space=pl.ANY)
    return pl.pallas_call(
        tie_kernel,
        out_shape=[jax.ShapeDtypeStruct(kept.shape, kept.dtype) for kept in (one, two)],
        in_specs=[anywhere, anywhere],
        out_specs=[anywhere, anywhere],
        input_output_aliases={0: 0, 1: 1},
        compiler_params=pltpu.CompilerParams(vmem_limit_bytes=limit),
        cost_estimate=cost(0, 0),
        name="order",
    )(one, two)


def merge_parts(first, second):
    max_one, total_one, numer_one = first
    level_two, mean_two = second
    largest = jnp.maximum(max_one, level_two)
    scale_one = jnp.exp(max_one - largest)
    scale_two = jnp.exp(level_two - largest)
    row_total = total_one * scale_one + scale_two
    numerator = numer_one * scale_one[..., None] + mean_two.astype(jnp.float32) * scale_two[..., None]
    merged = numerator / row_total[..., None]
    return merged.reshape(merged.shape[0], -1).astype(jnp.bfloat16)


def dispatch_kernel(
    ids_hbm, x_hbm, out_hbm, ids_ref, x_ref, stack_ref, first_ref, second_ref, out_ref, ids_sem, x_sem, out_sem
):
    ids_copy = pltpu.make_async_copy(ids_hbm, ids_ref, ids_sem)
    ids_copy.start()
    x_copy = pltpu.make_async_copy(x_hbm, x_ref, x_sem)
    x_copy.start()
    lane = lax.broadcasted_iota(jnp.int32, (ROW_BLOCK, LANES), 1)
    row = lax.broadcasted_iota(jnp.int32, (ROW_BLOCK, LANES), 0)
    spread = jnp.where(lane % ROW_BLOCK == row, 1.0, 0.0).astype(jnp.bfloat16)
    expert = lax.broadcasted_iota(jnp.int32, (EXPERTS, LANES), 0).astype(jnp.float32)
    ids_copy.wait()
    ids = ids_ref[...].astype(jnp.float32).astype(jnp.bfloat16)
    named = jnp.dot(ids, spread, preferred_element_type=jnp.float32)
    chosen = jnp.zeros((EXPERTS, LANES), jnp.float32)
    for choice in range(TOPK):
        chosen = jnp.where(expert == named[choice : choice + 1, :], 1.0, chosen)
    from_lane = lax.broadcasted_iota(jnp.int32, (LANES, LANES), 0)
    to_lane = lax.broadcasted_iota(jnp.int32, (LANES, LANES), 1)
    earlier = (from_lane // ROW_BLOCK == to_lane // ROW_BLOCK) & (from_lane < to_lane)
    rank = jnp.dot(
        chosen.astype(jnp.bfloat16),
        jnp.where(earlier, 1.0, 0.0).astype(jnp.bfloat16),
        preferred_element_type=jnp.float32,
    )
    first_ref[...] = jnp.where(rank == 0.0, chosen, 0.0)
    second_ref[...] = jnp.where(rank == 1.0, chosen, 0.0)
    sub = lax.broadcasted_iota(jnp.int32, (16, LANES), 0)
    sub_lane = lax.broadcasted_iota(jnp.int32, (16, LANES), 1)
    own_tile = sub_lane // ROW_BLOCK == sub // 2
    mask_first = jnp.where(own_tile & (sub % 2 == 0), 1.0, 0.0)
    mask_second = jnp.where(own_tile & (sub % 2 == 1), 1.0, 0.0)
    x_copy.wait()
    for tile in range(8):
        for group in range(GROUPS):
            column = (group * 8 + tile) * LANES
            stack_ref[tile * 16 : (tile + 1) * 16, group * LANES : (group + 1) * LANES] = x_ref[
                :, column : column + LANES
            ]
    stacked = stack_ref[...]
    per_piece = EXPERTS // PREP_PIECES

    def out_copy(piece):
        part = pl.ds(piece * per_piece, per_piece)
        return pltpu.make_async_copy(out_ref.at[part], out_hbm.at[part], out_sem.at[piece])

    for piece in range(PREP_PIECES):
        pickers = []
        for expert_at in range(piece * per_piece, (piece + 1) * per_piece):
            one = first_ref[expert_at : expert_at + 1, :]
            two = second_ref[expert_at : expert_at + 1, :]
            pickers.append((one * mask_first + two * mask_second).astype(jnp.bfloat16))
        picker = jnp.concatenate(pickers, axis=0)
        rows = jnp.dot(picker, stacked, preferred_element_type=jnp.float32).astype(jnp.bfloat16)
        for group in range(GROUPS):
            out_ref[
                piece * per_piece : (piece + 1) * per_piece, group * 16 : (group + 1) * 16, :
            ] = rows[:, group * LANES : (group + 1) * LANES].reshape(per_piece, 16, LANES)
        out_copy(piece).start()
    for piece in range(PREP_PIECES):
        out_copy(piece).wait()


def slot_shares_kernel(ids_ref, scores_ref, shares_ref):
    scores = scores_ref[...]
    shares = scores / jnp.sum(scores, axis=1, keepdims=True)
    ids = ids_ref[...]
    expert = lax.broadcasted_iota(jnp.int32, (ROW_BLOCK, EXPERTS), 1)
    chosen = jnp.zeros((ROW_BLOCK, EXPERTS), jnp.float32)
    share_of = jnp.zeros((ROW_BLOCK, EXPERTS), jnp.float32)
    for choice in range(TOPK):
        same = ids[:, choice : choice + 1] == expert
        chosen = jnp.where(same, 1.0, chosen)
        share_of = jnp.where(same, shares[:, choice : choice + 1], share_of)
    below = lax.broadcasted_iota(jnp.int32, (ROW_BLOCK, ROW_BLOCK), 1)
    above = lax.broadcasted_iota(jnp.int32, (ROW_BLOCK, ROW_BLOCK), 0)
    earlier = jnp.where(below < above, 1.0, 0.0).astype(jnp.bfloat16)
    rank = jnp.dot(earlier, chosen.astype(jnp.bfloat16), preferred_element_type=jnp.float32)
    slot_shares = jnp.concatenate(
        [jnp.where(rank == 0.0, share_of, 0.0), jnp.where(rank == 1.0, share_of, 0.0)], axis=1
    )
    high = slot_shares.astype(jnp.bfloat16)
    low = (slot_shares - high.astype(jnp.float32)).astype(jnp.bfloat16)
    shares_ref[...] = jnp.concatenate([high, low], axis=0)


def ffn_kernel(
    x_ref, gate_hbm, up_hbm, down_hbm, old_hbm, out_hbm,
    gate_ref, up_ref, down_ref, y_ref, rows_ref, in_sem, y_sem,
):
    span = DMODEL // GROUPS
    deep = DMODEL // FFN_PIECES

    def first_copies(piece):
        part = pl.ds(piece * deep, deep)
        return [
            pltpu.make_async_copy(gate_hbm.at[0, part, :], gate_ref.at[part, :], in_sem.at[0, piece]),
            pltpu.make_async_copy(up_hbm.at[0, part, :], up_ref.at[part, :], in_sem.at[1, piece]),
        ]

    def second_copies(piece):
        part = pl.ds(piece * deep, deep)
        return [pltpu.make_async_copy(down_hbm.at[0, :, part], down_ref.at[:, part], in_sem.at[2, piece])]

    queue = [first_copies(piece) for piece in range(FFN_PIECES)]
    queue += [second_copies(2 * pair) + second_copies(2 * pair + 1) for pair in range(FFN_PIECES // 2)]
    started = 0

    def start_until(count):
        nonlocal started
        while started < min(count, len(queue)):
            for copy in queue[started]:
                copy.start()
            started += 1

    def wait_for(index):
        for copy in queue[index]:
            copy.wait()
        start_until(index + 1 + FFN_AHEAD)

    def y_copy(group):
        return pltpu.make_async_copy(
            y_ref.at[group], out_hbm.at[:, pl.ds(group * 16, 16), :], y_sem.at[group]
        )

    start_until(FFN_AHEAD)
    out_row = lax.broadcasted_iota(jnp.int32, (LANES, LANES), 0)
    in_row = lax.broadcasted_iota(jnp.int32, (LANES, LANES), 1)
    gathered_from = (out_row // 2 % 8) * 16 + (out_row // 16) * 2 + out_row % 2
    swap = jnp.where(in_row == gathered_from, 1.0, 0.0).astype(jnp.bfloat16)

    for group in range(GROUPS):
        for block in range(0, 16, 2):
            pair = jnp.concatenate(
                [
                    x_ref[(block + i) * 8 : (block + i + 1) * 8, group * 16 : (group + 1) * 16].reshape(LANES, LANES)
                    for i in range(2)
                ],
                axis=1,
            )
            moved = jnp.dot(swap, pair, preferred_element_type=jnp.float32).astype(jnp.bfloat16)
            for tile in range(8):
                column = group * span + tile * LANES
                for i in range(2):
                    rows_ref[(block + i) * 16 : (block + i + 1) * 16, column : column + LANES] = moved[
                        tile * 16 : (tile + 1) * 16, i * LANES : (i + 1) * LANES
                    ]
    gate = up = None
    for piece in range(FFN_PIECES):
        wait_for(piece)
        part = slice(piece * deep, (piece + 1) * deep)
        rows = rows_ref[:, part]
        gate_part = jnp.dot(rows, gate_ref[part, :], preferred_element_type=jnp.float32)
        up_part = jnp.dot(rows, up_ref[part, :], preferred_element_type=jnp.float32)
        gate = gate_part if gate is None else gate + gate_part
        up = up_part if up is None else up + up_part
    hidden = (gate / (1.0 + jnp.exp(-gate)) * up).astype(jnp.bfloat16)
    for group in range(GROUPS):
        part = slice(group * span, (group + 1) * span)
        for piece in range(group * FFN_PIECES // 8, (group + 1) * FFN_PIECES // 8):
            wait_for(FFN_PIECES + piece)
        rows_ref[:, part] = jnp.dot(
            hidden, down_ref[:, part], preferred_element_type=jnp.float32
        ).astype(jnp.bfloat16)
        for block in range(0, 16, 2):
            pair = jnp.concatenate(
                [
                    jnp.concatenate(
                        [
                            rows_ref[
                                (block + i) * 16 : (block + i + 1) * 16,
                                group * span + tile * LANES : group * span + (tile + 1) * LANES,
                            ]
                            for tile in range(8)
                        ],
                        axis=0,
                    )
                    for i in range(2)
                ],
                axis=1,
            )
            moved = jnp.dot(swap, pair, preferred_element_type=jnp.float32).astype(jnp.bfloat16)
            for i in range(2):
                y_ref[group, (block + i) * 8 : (block + i + 1) * 8] = moved[
                    :, i * LANES : (i + 1) * LANES
                ].reshape(8, 16, LANES)
        y_copy(group).start()
    for group in range(GROUPS):
        y_copy(group).wait()


def combine_kernel(shares_ref, back_ref, out_ref, table_ref):
    both = shares_ref[...]
    piece = 512
    for start in range(0, EXPERTS * 16, piece):
        source = lax.broadcasted_iota(jnp.int32, (2 * EXPERTS, piece), 0)
        target = lax.broadcasted_iota(jnp.int32, (2 * EXPERTS, piece), 1) + start
        wanted = (target % 2) * EXPERTS + target // 16
        spread = jnp.where(source == wanted, 1.0, 0.0).astype(jnp.bfloat16)
        wide = jnp.dot(both, spread, preferred_element_type=jnp.float32)
        tile_of = (lax.broadcasted_iota(jnp.int32, (ROW_BLOCK, piece), 1) // 2) % 8
        for part in range(2):
            rows = wide[part * ROW_BLOCK : (part + 1) * ROW_BLOCK, :]
            for tile in range(8):
                at = part * LANES + tile * ROW_BLOCK
                table_ref[at : at + ROW_BLOCK, start : start + piece] = jnp.where(
                    tile_of == tile, rows, 0.0
                ).astype(jnp.bfloat16)
    back = jnp.concatenate(
        [
            back_ref[:, group * 16 : (group + 1) * 16, :].reshape(EXPERTS * 16, LANES)
            for group in range(GROUPS)
        ],
        axis=1,
    )
    total = jnp.dot(table_ref[...], back, preferred_element_type=jnp.float32)
    summed = total[:LANES, :] + total[LANES:, :]
    for tile in range(8):
        for group in range(GROUPS):
            column = (group * 8 + tile) * LANES
            out_ref[:, column : column + LANES] = summed[
                tile * 16 : (tile + 1) * 16, group * LANES : (group + 1) * LANES
            ].astype(jnp.bfloat16)


def whole():
    return pl.BlockSpec(memory_space=pltpu.VMEM)


def cost(flops, moved):
    return pl.CostEstimate(flops=flops, bytes_accessed=moved, transcendentals=0)


def dispatched(moe_input, expert_ids, route_scores):
    exchange = jax.ShapeDtypeStruct((EXPERTS, CHUNK, LANES), jnp.bfloat16)
    in_hbm = pl.BlockSpec(memory_space=pltpu.HBM)
    outgoing = pl.pallas_call(
        dispatch_kernel,
        out_shape=exchange,
        in_specs=[in_hbm, in_hbm],
        out_specs=in_hbm,
        scratch_shapes=[
            pltpu.VMEM((TOPK, ROW_BLOCK), jnp.int32),
            pltpu.VMEM((ROW_BLOCK, DMODEL), jnp.bfloat16),
            pltpu.VMEM((LANES, GROUPS * LANES), jnp.bfloat16),
            pltpu.VMEM((EXPERTS, LANES), jnp.float32),
            pltpu.VMEM((EXPERTS, LANES), jnp.float32),
            pltpu.VMEM((EXPERTS, CHUNK, LANES), jnp.bfloat16),
            pltpu.SemaphoreType.DMA,
            pltpu.SemaphoreType.DMA,
            pltpu.SemaphoreType.DMA((PREP_PIECES,)),
        ],
        compiler_params=pltpu.CompilerParams(vmem_limit_bytes=ALL_VMEM),
        cost_estimate=cost(300_000_000, 2_300_000),
        name="dispatch_rows",
    )(expert_ids.T, moe_input)
    arrived = lax.all_to_all(outgoing, ("grp", "dev"), split_axis=0, concat_axis=0, tiled=True)
    slot_shares = pl.pallas_call(
        slot_shares_kernel,
        out_shape=jax.ShapeDtypeStruct((2 * ROW_BLOCK, 2 * EXPERTS), jnp.bfloat16),
        in_specs=[whole(), whole()],
        out_specs=whole(),
        compiler_params=pltpu.CompilerParams(vmem_limit_bytes=16 << 20),
        cost_estimate=cost(1_000_000, 20_000),
        name="slot_shares",
    )(expert_ids, route_scores)
    return outgoing, arrived, slot_shares


def expert_answers(arrived, w_gate, w_up, w_down, outgoing):
    in_hbm = pl.BlockSpec(memory_space=pltpu.HBM)
    return pl.pallas_call(
        ffn_kernel,
        out_shape=jax.ShapeDtypeStruct((EXPERTS, CHUNK, LANES), jnp.bfloat16),
        in_specs=[whole()] + [in_hbm] * 4,
        out_specs=in_hbm,
        input_output_aliases={4: 0},
        scratch_shapes=[
            pltpu.VMEM((DMODEL, FF), jnp.bfloat16),
            pltpu.VMEM((DMODEL, FF), jnp.bfloat16),
            pltpu.VMEM((FF, DMODEL), jnp.bfloat16),
            pltpu.VMEM((GROUPS, EXPERTS, 16, LANES), jnp.bfloat16),
            pltpu.VMEM((2 * EXPERTS, DMODEL), jnp.bfloat16),
            pltpu.SemaphoreType.DMA((3, FFN_PIECES)),
            pltpu.SemaphoreType.DMA((GROUPS,)),
        ],
        compiler_params=pltpu.CompilerParams(vmem_limit_bytes=FFN_VMEM),
        cost_estimate=cost(4_800_000_000, 23_000_000),
        name="expert_ffn",
    )(arrived, w_gate, w_up, w_down, outgoing)


def collected(answers, slot_shares):
    returned = lax.all_to_all(answers, ("grp", "dev"), split_axis=0, concat_axis=0, tiled=True)
    return pl.pallas_call(
        combine_kernel,
        out_shape=jax.ShapeDtypeStruct((ROW_BLOCK, DMODEL), jnp.bfloat16),
        in_specs=[whole(), whole()],
        out_specs=whole(),
        scratch_shapes=[pltpu.VMEM((2 * LANES, EXPERTS * 16), jnp.bfloat16)],
        compiler_params=pltpu.CompilerParams(vmem_limit_bytes=16 << 20),
        cost_estimate=cost(540_000_000, 3_300_000),
        name="weighted_sum",
    )(slot_shares, returned)


def body(
    queries,
    cache_keys,
    cache_values,
    own_len,
    ext_keys,
    ext_values,
    ext_len,
    new_key,
    new_value,
    moe_input,
    expert_ids,
    route_scores,
    w_gate,
    w_up,
    w_down,
):
    slot_count = cache_keys.shape[1]
    positions = jnp.arange(slot_count + 1, dtype=jnp.int32)[None, :]
    own_live = (positions < own_len[:, None]) | (positions == slot_count)
    own_keys = jnp.concatenate([cache_keys, new_key[:, None, :]], axis=1)
    own_values = jnp.concatenate([cache_values, new_value[:, None, :]], axis=1)
    own_part = partial_softmax(queries, own_keys, own_values, own_live)
    far_queries = partner(queries, "dev", 0)
    helped = partial_softmax(far_queries, ext_keys, ext_values, positions[:, :slot_count] < ext_len[:, None])
    packed = packed_part(helped)
    outgoing, arrived, slot_shares = dispatched(moe_input, expert_ids, route_scores)
    packed, arrived = tied(packed, arrived, TIE_VMEM)
    far_part = partner(packed, "dev", 0)
    answers, far_part = tied(expert_answers(arrived, w_gate, w_up, w_down, outgoing), far_part, LATE_TIE_VMEM)
    moe_out = collected(answers, slot_shares)
    attention_out = merge_parts(own_part, unpacked_part(far_part))
    return (attention_out, moe_out)


def solution(mesh):
    placed = (
        P(("grp", "dev"), None),
        P(("grp", "dev"), None, None),
        P(("grp", "dev"), None, None),
        P(("grp", "dev")),
        P(("grp", "dev"), None, None),
        P(("grp", "dev"), None, None),
        P(("grp", "dev")),
        P(("grp", "dev"), None),
        P(("grp", "dev"), None),
        P(("grp", "dev"), None),
        P(("grp", "dev"), None),
        P(("grp", "dev"), None),
        P(("grp", "dev"), None, None),
        P(("grp", "dev"), None, None),
        P(("grp", "dev"), None, None),
    )
    return jax.shard_map(
        body,
        mesh=mesh,
        in_specs=placed,
        out_specs=(P(("grp", "dev"), None), P(("grp", "dev"), None)),
        check_vma=False,
    )
```

```python
import jax
import jax.numpy as jnp
from jax import lax
from jax.experimental import pallas as pl
from jax.experimental.pallas import tpu as pltpu
from jax.sharding import PartitionSpec as P

QH = 64
KVH = 4
HD = 128
DMODEL = 4096
FF = 768
TOPK = 8
EXPERTS = 128
ROW_BLOCK = 16
LANES = 128
GROUPS = 4
CHUNK = 64
PREP_PIECES = 8
FFN_PIECES = 8
FFN_AHEAD = 4
ALL_VMEM = 60 << 20
FFN_VMEM = 48 << 20
LATE_TIE_VMEM = 16 << 20


def partner(block, axis, apart):
    count = lax.axis_size(axis)
    route = []
    for low in range(count):
        high = low | 1 << apart
        if high != low and high < count:
            route += [(low, high), (high, low)]
    return lax.ppermute(block, axis, route)


def partial_softmax(queries, keys, values, live_slots):
    row_count = queries.shape[0]
    groups = QH // KVH
    query_flat = queries.astype(jnp.float32).reshape(row_count, KVH, groups, HD)
    key_flat = keys.astype(jnp.float32).reshape(row_count, keys.shape[1], KVH, HD)
    value_flat = values.astype(jnp.float32).reshape(row_count, values.shape[1], KVH, HD)
    scores = jnp.einsum("rkgh,rskh->rkgs", query_flat, key_flat) / jnp.sqrt(jnp.float32(HD))
    live_mask = live_slots[:, None, None, :]
    row_max = jnp.max(jnp.where(live_mask, scores, -jnp.inf), axis=-1)
    row_max = jnp.where(jnp.isfinite(row_max), row_max, -1e30)
    weights = jnp.where(live_mask, jnp.exp(scores - row_max[..., None]), 0.0)
    row_total = jnp.sum(weights, axis=-1)
    numerator = jnp.einsum("rkgs,rskh->rkgh", weights, value_flat)
    return (
        row_max.reshape(row_count, QH),
        row_total.reshape(row_count, QH),
        numerator.reshape(row_count, QH, HD),
    )


def packed_part(part):
    row_max, row_total, numerator = part
    live = row_total > 0.0
    safe = jnp.where(live, row_total, 1.0)
    level = jnp.where(live, row_max + jnp.log(safe), -1e30)
    high = lax.reduce_precision(level, 8, 7)
    middle = lax.reduce_precision(level - high, 8, 7)
    low = level - high - middle
    levels = jnp.concatenate([high, middle, low, jnp.zeros_like(low)], axis=1)
    mean = numerator / safe[..., None]
    return jnp.concatenate([mean, levels.reshape(-1, 2, HD)], axis=1).astype(jnp.bfloat16)


def unpacked_part(packed):
    levels = packed[:, QH:].reshape(-1, 4, QH).astype(jnp.float32)
    return levels[:, 0] + levels[:, 1] + levels[:, 2], packed[:, :QH]


def tie_kernel(one_ref, two_ref, one_out_ref, two_out_ref):
    pass


def tied(one, two, limit):
    anywhere = pl.BlockSpec(memory_space=pl.ANY)
    return pl.pallas_call(
        tie_kernel,
        out_shape=[jax.ShapeDtypeStruct(kept.shape, kept.dtype) for kept in (one, two)],
        in_specs=[anywhere, anywhere],
        out_specs=[anywhere, anywhere],
        input_output_aliases={0: 0, 1: 1},
        compiler_params=pltpu.CompilerParams(vmem_limit_bytes=limit),
        cost_estimate=cost(0, 0),
        name="order",
    )(one, two)


def merge_parts(first, second):
    max_one, total_one, numer_one = first
    level_two, mean_two = second
    largest = jnp.maximum(max_one, level_two)
    scale_one = jnp.exp(max_one - largest)
    scale_two = jnp.exp(level_two - largest)
    row_total = total_one * scale_one + scale_two
    numerator = numer_one * scale_one[..., None] + mean_two.astype(jnp.float32) * scale_two[..., None]
    merged = numerator / row_total[..., None]
    return merged.reshape(merged.shape[0], -1).astype(jnp.bfloat16)


def dispatch_kernel(
    ids_hbm, x_hbm, out_hbm, ids_ref, x_ref, stack_ref, first_ref, second_ref, out_ref, ids_sem, x_sem, out_sem
):
    ids_copy = pltpu.make_async_copy(ids_hbm, ids_ref, ids_sem)
    ids_copy.start()
    x_copy = pltpu.make_async_copy(x_hbm, x_ref, x_sem)
    x_copy.start()
    lane = lax.broadcasted_iota(jnp.int32, (ROW_BLOCK, LANES), 1)
    row = lax.broadcasted_iota(jnp.int32, (ROW_BLOCK, LANES), 0)
    spread = jnp.where(lane % ROW_BLOCK == row, 1.0, 0.0).astype(jnp.bfloat16)
    expert = lax.broadcasted_iota(jnp.int32, (EXPERTS, LANES), 0).astype(jnp.float32)
    ids_copy.wait()
    ids = ids_ref[...].astype(jnp.float32).astype(jnp.bfloat16)
    named = jnp.dot(ids, spread, preferred_element_type=jnp.float32)
    chosen = jnp.zeros((EXPERTS, LANES), jnp.float32)
    for choice in range(TOPK):
        chosen = jnp.where(expert == named[choice : choice + 1, :], 1.0, chosen)
    from_lane = lax.broadcasted_iota(jnp.int32, (LANES, LANES), 0)
    to_lane = lax.broadcasted_iota(jnp.int32, (LANES, LANES), 1)
    earlier = (from_lane // ROW_BLOCK == to_lane // ROW_BLOCK) & (from_lane < to_lane)
    rank = jnp.dot(
        chosen.astype(jnp.bfloat16),
        jnp.where(earlier, 1.0, 0.0).astype(jnp.bfloat16),
        preferred_element_type=jnp.float32,
    )
    first_ref[...] = jnp.where(rank == 0.0, chosen, 0.0)
    second_ref[...] = jnp.where(rank == 1.0, chosen, 0.0)
    sub = lax.broadcasted_iota(jnp.int32, (16, LANES), 0)
    sub_lane = lax.broadcasted_iota(jnp.int32, (16, LANES), 1)
    own_tile = sub_lane // ROW_BLOCK == sub // 2
    mask_first = jnp.where(own_tile & (sub % 2 == 0), 1.0, 0.0)
    mask_second = jnp.where(own_tile & (sub % 2 == 1), 1.0, 0.0)
    x_copy.wait()
    for tile in range(8):
        for group in range(GROUPS):
            column = (group * 8 + tile) * LANES
            stack_ref[tile * 16 : (tile + 1) * 16, group * LANES : (group + 1) * LANES] = x_ref[
                :, column : column + LANES
            ]
    stacked = stack_ref[...]
    per_piece = EXPERTS // PREP_PIECES

    def out_copy(piece):
        part = pl.ds(piece * per_piece, per_piece)
        return pltpu.make_async_copy(out_ref.at[part], out_hbm.at[part], out_sem.at[piece])

    for piece in range(PREP_PIECES):
        pickers = []
        for expert_at in range(piece * per_piece, (piece + 1) * per_piece):
            one = first_ref[expert_at : expert_at + 1, :]
            two = second_ref[expert_at : expert_at + 1, :]
            pickers.append((one * mask_first + two * mask_second).astype(jnp.bfloat16))
        picker = jnp.concatenate(pickers, axis=0)
        rows = jnp.dot(picker, stacked, preferred_element_type=jnp.float32).astype(jnp.bfloat16)
        for group in range(GROUPS):
            out_ref[
                piece * per_piece : (piece + 1) * per_piece, group * 16 : (group + 1) * 16, :
            ] = rows[:, group * LANES : (group + 1) * LANES].reshape(per_piece, 16, LANES)
        out_copy(piece).start()
    for piece in range(PREP_PIECES):
        out_copy(piece).wait()


def slot_shares_kernel(ids_ref, scores_ref, shares_ref):
    scores = scores_ref[...]
    shares = scores / jnp.sum(scores, axis=1, keepdims=True)
    ids = ids_ref[...]
    expert = lax.broadcasted_iota(jnp.int32, (ROW_BLOCK, EXPERTS), 1)
    chosen = jnp.zeros((ROW_BLOCK, EXPERTS), jnp.float32)
    share_of = jnp.zeros((ROW_BLOCK, EXPERTS), jnp.float32)
    for choice in range(TOPK):
        same = ids[:, choice : choice + 1] == expert
        chosen = jnp.where(same, 1.0, chosen)
        share_of = jnp.where(same, shares[:, choice : choice + 1], share_of)
    below = lax.broadcasted_iota(jnp.int32, (ROW_BLOCK, ROW_BLOCK), 1)
    above = lax.broadcasted_iota(jnp.int32, (ROW_BLOCK, ROW_BLOCK), 0)
    earlier = jnp.where(below < above, 1.0, 0.0).astype(jnp.bfloat16)
    rank = jnp.dot(earlier, chosen.astype(jnp.bfloat16), preferred_element_type=jnp.float32)
    slot_shares = jnp.concatenate(
        [jnp.where(rank == 0.0, share_of, 0.0), jnp.where(rank == 1.0, share_of, 0.0)], axis=1
    )
    high = slot_shares.astype(jnp.bfloat16)
    low = (slot_shares - high.astype(jnp.float32)).astype(jnp.bfloat16)
    shares_ref[...] = jnp.concatenate([high, low], axis=0)


def ffn_kernel(
    x_ref, gate_hbm, up_hbm, down_hbm, old_hbm, out_hbm,
    gate_ref, up_ref, down_ref, y_ref, rows_ref, in_sem, y_sem,
):
    span = DMODEL // GROUPS
    deep = DMODEL // FFN_PIECES

    def first_copies(piece):
        part = pl.ds(piece * deep, deep)
        return [
            pltpu.make_async_copy(gate_hbm.at[0, part, :], gate_ref.at[part, :], in_sem.at[0, piece]),
            pltpu.make_async_copy(up_hbm.at[0, part, :], up_ref.at[part, :], in_sem.at[1, piece]),
        ]

    def second_copies(piece):
        part = pl.ds(piece * deep, deep)
        return [pltpu.make_async_copy(down_hbm.at[0, :, part], down_ref.at[:, part], in_sem.at[2, piece])]

    queue = [first_copies(piece) for piece in range(FFN_PIECES)]
    queue += [second_copies(2 * pair) + second_copies(2 * pair + 1) for pair in range(FFN_PIECES // 2)]
    started = 0

    def start_until(count):
        nonlocal started
        while started < min(count, len(queue)):
            for copy in queue[started]:
                copy.start()
            started += 1

    def wait_for(index):
        for copy in queue[index]:
            copy.wait()
        start_until(index + 1 + FFN_AHEAD)

    def y_copy(group):
        return pltpu.make_async_copy(
            y_ref.at[group], out_hbm.at[:, pl.ds(group * 16, 16), :], y_sem.at[group]
        )

    start_until(FFN_AHEAD)
    out_row = lax.broadcasted_iota(jnp.int32, (LANES, LANES), 0)
    in_row = lax.broadcasted_iota(jnp.int32, (LANES, LANES), 1)
    gathered_from = (out_row // 2 % 8) * 16 + (out_row // 16) * 2 + out_row % 2
    swap = jnp.where(in_row == gathered_from, 1.0, 0.0).astype(jnp.bfloat16)

    for group in range(GROUPS):
        for block in range(0, 16, 2):
            pair = jnp.concatenate(
                [
                    x_ref[(block + i) * 8 : (block + i + 1) * 8, group * 16 : (group + 1) * 16].reshape(LANES, LANES)
                    for i in range(2)
                ],
                axis=1,
            )
            moved = jnp.dot(swap, pair, preferred_element_type=jnp.float32).astype(jnp.bfloat16)
            for tile in range(8):
                column = group * span + tile * LANES
                for i in range(2):
                    rows_ref[(block + i) * 16 : (block + i + 1) * 16, column : column + LANES] = moved[
                        tile * 16 : (tile + 1) * 16, i * LANES : (i + 1) * LANES
                    ]
    gate = up = None
    for piece in range(FFN_PIECES):
        wait_for(piece)
        part = slice(piece * deep, (piece + 1) * deep)
        rows = rows_ref[:, part]
        gate_part = jnp.dot(rows, gate_ref[part, :], preferred_element_type=jnp.float32)
        up_part = jnp.dot(rows, up_ref[part, :], preferred_element_type=jnp.float32)
        gate = gate_part if gate is None else gate + gate_part
        up = up_part if up is None else up + up_part
    hidden = (gate / (1.0 + jnp.exp(-gate)) * up).astype(jnp.bfloat16)
    for group in range(GROUPS):
        part = slice(group * span, (group + 1) * span)
        for piece in range(group * FFN_PIECES // 8, (group + 1) * FFN_PIECES // 8):
            wait_for(FFN_PIECES + piece)
        rows_ref[:, part] = jnp.dot(
            hidden, down_ref[:, part], preferred_element_type=jnp.float32
        ).astype(jnp.bfloat16)
        for block in range(0, 16, 2):
            pair = jnp.concatenate(
                [
                    jnp.concatenate(
                        [
                            rows_ref[
                                (block + i) * 16 : (block + i + 1) * 16,
                                group * span + tile * LANES : group * span + (tile + 1) * LANES,
                            ]
                            for tile in range(8)
                        ],
                        axis=0,
                    )
                    for i in range(2)
                ],
                axis=1,
            )
            moved = jnp.dot(swap, pair, preferred_element_type=jnp.float32).astype(jnp.bfloat16)
            for i in range(2):
                y_ref[group, (block + i) * 8 : (block + i + 1) * 8] = moved[
                    :, i * LANES : (i + 1) * LANES
                ].reshape(8, 16, LANES)
        y_copy(group).start()
    for group in range(GROUPS):
        y_copy(group).wait()


def combine_kernel(shares_ref, back_ref, out_ref, table_ref):
    both = shares_ref[...]
    piece = 512
    for start in range(0, EXPERTS * 16, piece):
        source = lax.broadcasted_iota(jnp.int32, (2 * EXPERTS, piece), 0)
        target = lax.broadcasted_iota(jnp.int32, (2 * EXPERTS, piece), 1) + start
        wanted = (target % 2) * EXPERTS + target // 16
        spread = jnp.where(source == wanted, 1.0, 0.0).astype(jnp.bfloat16)
        wide = jnp.dot(both, spread, preferred_element_type=jnp.float32)
        tile_of = (lax.broadcasted_iota(jnp.int32, (ROW_BLOCK, piece), 1) // 2) % 8
        for part in range(2):
            rows = wide[part * ROW_BLOCK : (part + 1) * ROW_BLOCK, :]
            for tile in range(8):
                at = part * LANES + tile * ROW_BLOCK
                table_ref[at : at + ROW_BLOCK, start : start + piece] = jnp.where(
                    tile_of == tile, rows, 0.0
                ).astype(jnp.bfloat16)
    back = jnp.concatenate(
        [
            back_ref[:, group * 16 : (group + 1) * 16, :].reshape(EXPERTS * 16, LANES)
            for group in range(GROUPS)
        ],
        axis=1,
    )
    total = jnp.dot(table_ref[...], back, preferred_element_type=jnp.float32)
    summed = total[:LANES, :] + total[LANES:, :]
    for tile in range(8):
        for group in range(GROUPS):
            column = (group * 8 + tile) * LANES
            out_ref[:, column : column + LANES] = summed[
                tile * 16 : (tile + 1) * 16, group * LANES : (group + 1) * LANES
            ].astype(jnp.bfloat16)


def whole():
    return pl.BlockSpec(memory_space=pltpu.VMEM)


def cost(flops, moved):
    return pl.CostEstimate(flops=flops, bytes_accessed=moved, transcendentals=0)


def dispatched(moe_input, expert_ids, route_scores):
    exchange = jax.ShapeDtypeStruct((EXPERTS, CHUNK, LANES), jnp.bfloat16)
    in_hbm = pl.BlockSpec(memory_space=pltpu.HBM)
    outgoing = pl.pallas_call(
        dispatch_kernel,
        out_shape=exchange,
        in_specs=[in_hbm, in_hbm],
        out_specs=in_hbm,
        scratch_shapes=[
            pltpu.VMEM((TOPK, ROW_BLOCK), jnp.int32),
            pltpu.VMEM((ROW_BLOCK, DMODEL), jnp.bfloat16),
            pltpu.VMEM((LANES, GROUPS * LANES), jnp.bfloat16),
            pltpu.VMEM((EXPERTS, LANES), jnp.float32),
            pltpu.VMEM((EXPERTS, LANES), jnp.float32),
            pltpu.VMEM((EXPERTS, CHUNK, LANES), jnp.bfloat16),
            pltpu.SemaphoreType.DMA,
            pltpu.SemaphoreType.DMA,
            pltpu.SemaphoreType.DMA((PREP_PIECES,)),
        ],
        compiler_params=pltpu.CompilerParams(vmem_limit_bytes=ALL_VMEM),
        cost_estimate=cost(300_000_000, 2_300_000),
        name="dispatch_rows",
    )(expert_ids.T, moe_input)
    arrived = lax.all_to_all(outgoing, ("grp", "dev"), split_axis=0, concat_axis=0, tiled=True)
    slot_shares = pl.pallas_call(
        slot_shares_kernel,
        out_shape=jax.ShapeDtypeStruct((2 * ROW_BLOCK, 2 * EXPERTS), jnp.bfloat16),
        in_specs=[whole(), whole()],
        out_specs=whole(),
        compiler_params=pltpu.CompilerParams(vmem_limit_bytes=16 << 20),
        cost_estimate=cost(1_000_000, 20_000),
        name="slot_shares",
    )(expert_ids, route_scores)
    return outgoing, arrived, slot_shares


def expert_answers(arrived, w_gate, w_up, w_down, outgoing):
    in_hbm = pl.BlockSpec(memory_space=pltpu.HBM)
    return pl.pallas_call(
        ffn_kernel,
        out_shape=jax.ShapeDtypeStruct((EXPERTS, CHUNK, LANES), jnp.bfloat16),
        in_specs=[whole()] + [in_hbm] * 4,
        out_specs=in_hbm,
        input_output_aliases={4: 0},
        scratch_shapes=[
            pltpu.VMEM((DMODEL, FF), jnp.bfloat16),
            pltpu.VMEM((DMODEL, FF), jnp.bfloat16),
            pltpu.VMEM((FF, DMODEL), jnp.bfloat16),
            pltpu.VMEM((GROUPS, EXPERTS, 16, LANES), jnp.bfloat16),
            pltpu.VMEM((2 * EXPERTS, DMODEL), jnp.bfloat16),
            pltpu.SemaphoreType.DMA((3, FFN_PIECES)),
            pltpu.SemaphoreType.DMA((GROUPS,)),
        ],
        compiler_params=pltpu.CompilerParams(vmem_limit_bytes=FFN_VMEM),
        cost_estimate=cost(4_800_000_000, 23_000_000),
        name="expert_ffn",
    )(arrived, w_gate, w_up, w_down, outgoing)


def collected(answers, slot_shares):
    returned = lax.all_to_all(answers, ("grp", "dev"), split_axis=0, concat_axis=0, tiled=True)
    return pl.pallas_call(
        combine_kernel,
        out_shape=jax.ShapeDtypeStruct((ROW_BLOCK, DMODEL), jnp.bfloat16),
        in_specs=[whole(), whole()],
        out_specs=whole(),
        scratch_shapes=[pltpu.VMEM((2 * LANES, EXPERTS * 16), jnp.bfloat16)],
        compiler_params=pltpu.CompilerParams(vmem_limit_bytes=16 << 20),
        cost_estimate=cost(540_000_000, 3_300_000),
        name="weighted_sum",
    )(slot_shares, returned)


def body(
    queries,
    cache_keys,
    cache_values,
    own_len,
    ext_keys,
    ext_values,
    ext_len,
    new_key,
    new_value,
    moe_input,
    expert_ids,
    route_scores,
    w_gate,
    w_up,
    w_down,
):
    slot_count = cache_keys.shape[1]
    positions = jnp.arange(slot_count + 1, dtype=jnp.int32)[None, :]
    own_live = (positions < own_len[:, None]) | (positions == slot_count)
    own_keys = jnp.concatenate([cache_keys, new_key[:, None, :]], axis=1)
    own_values = jnp.concatenate([cache_values, new_value[:, None, :]], axis=1)
    own_part = partial_softmax(queries, own_keys, own_values, own_live)
    far_queries = partner(queries, "dev", 0)
    helped = partial_softmax(far_queries, ext_keys, ext_values, positions[:, :slot_count] < ext_len[:, None])
    packed = packed_part(helped)
    outgoing, arrived, slot_shares = dispatched(moe_input, expert_ids, route_scores)
    far_part = partner(packed, "dev", 0)
    answers, far_part = tied(expert_answers(arrived, w_gate, w_up, w_down, outgoing), far_part, LATE_TIE_VMEM)
    moe_out = collected(answers, slot_shares)
    attention_out = merge_parts(own_part, unpacked_part(far_part))
    return (attention_out, moe_out)


def solution(mesh):
    placed = (
        P(("grp", "dev"), None),
        P(("grp", "dev"), None, None),
        P(("grp", "dev"), None, None),
        P(("grp", "dev")),
        P(("grp", "dev"), None, None),
        P(("grp", "dev"), None, None),
        P(("grp", "dev")),
        P(("grp", "dev"), None),
        P(("grp", "dev"), None),
        P(("grp", "dev"), None),
        P(("grp", "dev"), None),
        P(("grp", "dev"), None),
        P(("grp", "dev"), None, None),
        P(("grp", "dev"), None, None),
        P(("grp", "dev"), None, None),
    )
    return jax.shard_map(
        body,
        mesh=mesh,
        in_specs=placed,
        out_specs=(P(("grp", "dev"), None), P(("grp", "dev"), None)),
        check_vma=False,
    )
```
